32 devices in a mesh: ctx: 8 (over y, x, core), seq: 4 (over z).
Axes of the slice: x: 2, y: 2, z: 4, core: 2. Of those that a mesh axis runs over, the one named last changes fastest.
Arguments:
- residual_in: bfloat16 [4, 1024, 2048], P('seq', 'ctx'), may hold values from -6 to 6
- query_in: bfloat16 [4, 1024, 1024], P('seq', 'ctx'), may hold values from -6 to 6
- key_in: bfloat16 [4, 1024, 1024], P('seq', 'ctx'), may hold values from -6 to 6
- value_in: bfloat16 [4, 1024, 2048], P('seq', 'ctx'), may hold values from -6 to 6
- gate_in: bfloat16 [4, 1024, 2048], P('seq', 'ctx'), may hold values from -6 to 6
- log_decay: float32 [4, 16, 1024], P('seq', None, 'ctx'), may hold values from -0.8 to 0
- write_rate: float32 [4, 16, 1024], P('seq', None, 'ctx'), may hold values from 0.003 to 0.9
- state_start: float32 [4, 16, 128, 128], P('seq'), may hold values from -0.2 to 0.2
- head_gain: float32 [128], replicated, may hold values from 0.1 to 1.9
- out_proj: bfloat16 [2048, 2048], replicated, may hold values from -0.125 to 0.125
- moe_gain: float32 [2048], replicated, may hold values from 0.1 to 1.9
- expert_in: bfloat16 [64, 2048, 1024], P(('ctx', 'seq')), may hold values from -0.125 to 0.125
- expert_out: bfloat16 [64, 512, 2048], P(('ctx', 'seq')), may hold values from -0.25 to 0.25
- route_ids: int32 [4, 1024, 10], P('seq', 'ctx'), may hold values from 0 to 63, all different within a row; in each aligned block of 128 rows (0 to 127, 128 to 255, ..., all dimensions but the last counted through in order) at most 48 rows name the same one
- route_probs: float32 [4, 1024, 10], P('seq', 'ctx'), may hold values from 0.01 to 1
Outputs:
- layer_out: bfloat16 [4, 1024, 2048], P('seq', 'ctx')
The draws below stay inside these ranges and needn't reach their ends.
Inputs may be any that keep to these rules, and one draw needn't show every extreme that they name: `route_ids`: within the 128 rows of one device no expert is named more than 48 times, a bound that some block reaches; the 10 experts of a token differ.
All inputs are finite; a program needn't handle non-finite values.
Results may differ from the reference program's by a relative error of at most 0.01.
Values may be sent and summed in bfloat16 or wider, within the bound.
A program may use at most 192 MiB of HBM per device.

```python
import math
import jax
import jax.numpy as jnp
import numpy as np
from jax import lax

D = 2048
H = 16
KH = 8
DK = 128
DV = 128
GROUP = 64
FFE = 512
TOP = 10
TOK = 128
SEQUENCE_COUNT = 4
WINDOW_LENGTH = 1024
EXPERTS = 64
CAP = 48


def head_kinds(key):
    chosen = jax.random.uniform(jax.random.fold_in(key, 101), (SEQUENCE_COUNT, H, 1))
    slow_share = 0.5
    return jnp.where(chosen < slow_share, 1.0, 0.0).astype(jnp.float32)


def draw_log_decay(key, part):
    slow_heads = head_kinds(key)
    token_factor = jnp.exp(jax.random.uniform(jax.random.fold_in(key, 1), (SEQUENCE_COUNT, H, WINDOW_LENGTH), minval=-0.7, maxval=0.7))
    block_factor = jnp.exp(jax.random.uniform(jax.random.fold_in(key, 2), (SEQUENCE_COUNT, H, WINDOW_LENGTH // TOK), minval=-0.7, maxval=0.7))
    block_factor = jnp.repeat(block_factor, TOK, axis=2)
    learning_rates = (slow_heads * (0.1 / WINDOW_LENGTH) + (1.0 - slow_heads) * (1.0 / 40.0)) * token_factor * block_factor
    spike_position = jax.random.randint(jax.random.fold_in(key, 3), (SEQUENCE_COUNT, 2, 1), 0, WINDOW_LENGTH)
    token_positions = jnp.arange(WINDOW_LENGTH)[None, None, :]
    spike_events = jnp.any(token_positions == spike_position, axis=1, keepdims=True).astype(jnp.float32)
    loss_values = jax.random.uniform(jax.random.fold_in(key, 4), (SEQUENCE_COUNT, H, WINDOW_LENGTH), minval=0.22, maxval=0.69)
    return (-(learning_rates + spike_events * loss_values)).astype(jnp.float32)


def draw_write_rate(key, part):
    slow_heads = head_kinds(key)
    lower = jnp.exp(jax.random.uniform(jax.random.fold_in(key, 5), (SEQUENCE_COUNT, H, WINDOW_LENGTH), minval=math.log(0.003), maxval=math.log(0.02)))
    upper = jnp.exp(jax.random.uniform(jax.random.fold_in(key, 6), (SEQUENCE_COUNT, H, WINDOW_LENGTH), minval=math.log(0.2), maxval=math.log(0.9)))
    return (slow_heads * lower + (1.0 - slow_heads) * upper).astype(jnp.float32)


def shard_levels(stream_key, shape, shards, smallest, top_value):
    gain, own = 1.0, jax.random.fold_in(stream_key, 6)
    for position, blocks in shards:
        heights = jnp.exp(jax.random.uniform(jax.random.fold_in(own, position), (blocks,), jnp.float32, smallest / len(shards), top_value / len(shards)))
        gain = gain * jnp.repeat(heights, shape[position] // blocks).reshape([-1 if axis == position else 1 for axis in range(len(shape))])
    return gain


def shared_out(stream_key, own, number, rows, count, top, bound, lean):
    sequence = jax.random.permutation(stream_key, count)
    packed, common = portions_of(count, rows * top, bound, lean, True), portions_of(count, rows * top, bound, lean, False)
    places = jnp.arange(count)

    def named(tallies, offset_by):
        used = int((tallies > 0).sum())
        fixed = max(1, used // 4)
        passed = fixed + (places - fixed + offset_by * (used - fixed)) % max(1, count - fixed)
        return jnp.zeros((count,), jnp.int32).at[sequence[jnp.where(places < fixed, places, passed)]].set(jnp.asarray(tallies, jnp.int32))

    tallies = jnp.where(number % 4 == 0, named(packed, number // 4), named(common, number - number // 4 - 1))
    mixed = jax.random.permutation(jax.random.fold_in(own, 3), count)
    giver, taker = mixed[0:count // 2 * 2:2], mixed[1:count // 2 * 2:2]
    slack = jnp.minimum(tallies[giver] - 1, bound - tallies[taker]) // 2
    slack = jnp.where((giver == sequence[0]) | (taker == sequence[0]) | (tallies[taker] == 0), 0, jnp.maximum(slack, 0))
    passed = jax.random.randint(jax.random.fold_in(own, 4), (count // 2,), 0, 1 << 20) % (slack + 1)
    tallies = tallies.at[giver].add(-passed).at[taker].add(passed)
    items = jnp.searchsorted(jnp.cumsum(tallies), jnp.arange(rows * top), side="right").astype(jnp.int32)
    table = items.reshape(top, rows).T
    table = table[jax.random.permutation(jax.random.fold_in(own, 1), rows)]
    offset_by = jax.random.randint(jax.random.fold_in(own, 2), (rows, 1), 0, top)
    return jnp.take_along_axis(table, (jnp.arange(top)[None, :] + offset_by) % top, axis=1)


def portions_of(count, total, reach, skew, full):
    loads = [(1 << 20) // math.isqrt(grade ** skew) + 1 for grade in range(1, count + 1)]
    largest = reach if full else min(reach, max(-(-total // count), total * loads[0] // sum(loads)))
    least = 1 if total - largest >= count - 1 else 0
    holding, surplus = [largest] + [least] * (count - 1), total - largest - least * (count - 1)
    while surplus > 0:
        candidates = [i for i in range(1, count) if holding[i] < largest] or [i for i in range(1, count) if holding[i] < reach]
        mass, remaining = sum([loads[i] for i in candidates]), surplus
        for i in candidates:
            extra = min(reach - holding[i], max(1, remaining * loads[i] // mass), surplus)
            holding[i] = holding[i] + extra
            surplus = surplus - extra
    return np.array(holding)


def normal_values(stream_key, shape, width, most, split=(), held_as=jnp.bfloat16):
    drawn = jax.random.normal(stream_key, shape, jnp.float32) * width
    if len(split) > 0:
        drawn = shard_levels(stream_key, shape, split, -0.22, 0.18) * drawn
    return jnp.clip(drawn, min=-most, max=most).astype(held_as)


def setup_inputs(seed: int = 0) -> dict:
    key_of = jax.random.split(jax.random.key(seed), 16)
    residual_in = normal_values(key_of[0], (SEQUENCE_COUNT, WINDOW_LENGTH, D), 1.0, 6.0, ((0, 4), (1, 8)))
    query_in = normal_values(key_of[1], (SEQUENCE_COUNT, WINDOW_LENGTH, KH * DK), 1.0, 6.0, ((0, 4), (1, 8)))
    key_in = normal_values(key_of[2], (SEQUENCE_COUNT, WINDOW_LENGTH, KH * DK), 1.0, 6.0, ((0, 4), (1, 8)))
    value_in = normal_values(key_of[3], (SEQUENCE_COUNT, WINDOW_LENGTH, H * DV), 1.0, 6.0, ((0, 4), (1, 8)))
    gate_in = normal_values(key_of[4], (SEQUENCE_COUNT, WINDOW_LENGTH, H * DV), 1.0, 6.0, ((0, 4), (1, 8)))
    log_decay = draw_log_decay(jax.random.fold_in(key_of[15], 71), 0)
    write_rate = draw_write_rate(jax.random.fold_in(key_of[15], 71), 0)
    state_start = normal_values(key_of[7], (SEQUENCE_COUNT, H, DK, DV), 0.03, 0.2, ((0, 4),), jnp.float32)
    head_gain = jnp.clip(1.0 + 0.18 * jax.random.normal(key_of[8], (DV,), jnp.float32), 0.1, 1.9)
    out_proj = normal_values(key_of[9], (H * DV, D), (H * DV) ** -0.5, 0.125)
    moe_gain = jnp.clip(1.0 + 0.18 * jax.random.normal(key_of[10], (D,), jnp.float32), 0.1, 1.9)
    expert_in = normal_values(key_of[11], (EXPERTS, D, 2 * FFE), D ** -0.5, 0.125, ((0, 32),))
    expert_out = normal_values(key_of[12], (EXPERTS, FFE, D), FFE ** -0.5, 0.25, ((0, 32),))
    route_ids_keys = jax.random.split(jax.random.fold_in(key_of[13], 1), SEQUENCE_COUNT * WINDOW_LENGTH // TOK)
    route_ids_turns = jax.random.permutation(jax.random.fold_in(key_of[13], 3), SEQUENCE_COUNT * WINDOW_LENGTH // TOK)
    route_ids = jax.vmap(lambda own, number: shared_out(jax.random.fold_in(key_of[13], 2), own, number, TOK, EXPERTS, TOP, CAP, 2))(route_ids_keys, route_ids_turns).reshape((SEQUENCE_COUNT, WINDOW_LENGTH, TOP))
    route_probs = jnp.clip(jnp.exp(math.log(1.0) - 4.6051702 * jax.random.uniform(key_of[14], (SEQUENCE_COUNT, WINDOW_LENGTH, TOP), jnp.float32) ** shard_levels(key_of[14], (SEQUENCE_COUNT, WINDOW_LENGTH, TOP), ((0, 4), (1, 8)), -0.2, 0.2)), 0.01, 1.0)
    return {"residual_in": residual_in, "query_in": query_in, "key_in": key_in, "value_in": value_in, "gate_in": gate_in, "log_decay": log_decay, "write_rate": write_rate, "state_start": state_start, "head_gain": head_gain, "out_proj": out_proj, "moe_gain": moe_gain, "expert_in": expert_in, "expert_out": expert_out, "route_ids": route_ids, "route_probs": route_probs}


HIGHEST = lax.Precision.HIGHEST

def product(form, left, right):
    return jnp.einsum(form, left, right, precision=HIGHEST)

def unit_rows(values):
    return values * lax.rsqrt(lax.optimization_barrier(jnp.sum(values * values, axis=-1, keepdims=True)) + 1e-06)

def group_terms(query_rows, key_rows, value_rows, log_gates, strengths):
    length = log_gates.shape[-1]
    cumulative = jnp.cumsum(log_gates, axis=-1)
    log_gaps = cumulative[..., :, None] - cumulative[..., None, :]
    row_index = jnp.arange(length)[:, None]
    col_index = jnp.arange(length)[None, :]
    inclusive = col_index <= row_index
    strict = col_index < row_index
    decays = jnp.where(inclusive, jnp.exp(jnp.where(inclusive, log_gaps, 0.0)), 0.0)
    identity_c = jnp.eye(length, dtype=jnp.float32)
    identity_k = jnp.eye(key_rows.shape[-1], dtype=jnp.float32)
    couple = jnp.where(strict, strengths[..., :, None] * decays * product('...id,...jd->...ij', key_rows, key_rows), 0.0)
    inverse = identity_c - couple
    powers = couple
    extent = 2
    while extent < length:
        powers = product('...ij,...jk->...ik', powers, powers)
        inverse = product('...ij,...jk->...ik', inverse, identity_c + powers)
        extent = extent * 2
    gammas = jnp.exp(cumulative)
    pseudo = product('...ij,...jv->...iv', inverse, strengths[..., None] * value_rows)
    erased = product('...ij,...jd->...id', inverse, (strengths * gammas)[..., None] * key_rows)
    to_end = jnp.exp(cumulative[..., -1:] - cumulative)[..., None] * key_rows
    transfer = gammas[..., -1][..., None, None] * identity_k - product('...ci,...cj->...ij', to_end, erased)
    offset = product('...ci,...cv->...iv', to_end, pseudo)
    scores = decays * product('...id,...jd->...ij', query_rows, key_rows)
    local_out = product('...ij,...jv->...iv', scores, pseudo)
    reach_map = gammas[..., None] * query_rows - product('...ij,...jd->...id', scores, erased)
    return (transfer, offset, local_out, reach_map)

def delta_layer(query_in, key_in, value_in, log_decay, write_rate, state_start):
    repeat_by = H // KH
    group_count = WINDOW_LENGTH // GROUP
    queries = unit_rows(query_in.astype(jnp.float32).reshape(SEQUENCE_COUNT, WINDOW_LENGTH, KH, DK))
    key_rows = unit_rows(key_in.astype(jnp.float32).reshape(SEQUENCE_COUNT, WINDOW_LENGTH, KH, DK))
    queries = jnp.repeat(queries, repeat_by, axis=2).transpose(0, 2, 1, 3).reshape(SEQUENCE_COUNT, H, group_count, GROUP, DK)
    key_rows = jnp.repeat(key_rows, repeat_by, axis=2).transpose(0, 2, 1, 3).reshape(SEQUENCE_COUNT, H, group_count, GROUP, DK)
    value_rows = value_in.astype(jnp.float32).reshape(SEQUENCE_COUNT, WINDOW_LENGTH, H, DV).transpose(0, 2, 1, 3).reshape(SEQUENCE_COUNT, H, group_count, GROUP, DV)
    gates = log_decay.reshape(SEQUENCE_COUNT, H, group_count, GROUP)
    strengths = write_rate.reshape(SEQUENCE_COUNT, H, group_count, GROUP)
    pieces = (jnp.moveaxis(queries, 2, 0), jnp.moveaxis(key_rows, 2, 0), jnp.moveaxis(value_rows, 2, 0), jnp.moveaxis(gates, 2, 0), jnp.moveaxis(strengths, 2, 0))

    def advance(carried, group_pieces):
        transfer, offset, local_out, reach_map = group_terms(*group_pieces)
        outputs = local_out + product('shcd,shdv->shcv', reach_map, carried)
        carried = product('shij,shjv->shiv', transfer, carried) + offset
        return (carried, outputs)
    final_state, outputs = lax.scan(advance, state_start.astype(jnp.float32), pieces)
    return outputs.transpose(1, 0, 3, 2, 4).reshape(SEQUENCE_COUNT, WINDOW_LENGTH, H, DV)

def expert_layer(moe_in, expert_in, expert_out, route_ids, shares):
    pair_count = route_ids.shape[0] * route_ids.shape[1] * route_ids.shape[2]
    flat_ids = route_ids.reshape(-1).astype(jnp.int32)
    flat_shares = shares.reshape(-1)
    token_of = (jnp.arange(pair_count) // TOP).astype(jnp.int32)
    sorted_pairs = jnp.argsort(flat_ids, stable=True).astype(jnp.int32)
    counts = jnp.bincount(flat_ids, length=EXPERTS).astype(jnp.int32)
    starts = (jnp.cumsum(counts) - counts).astype(jnp.int32)
    block_rows = 128
    blocks_each = ((counts + block_rows - 1) // block_rows).astype(jnp.int32)
    block_starts = (jnp.cumsum(blocks_each) - blocks_each).astype(jnp.int32)
    block_total = -(-pair_count // block_rows) + EXPERTS

    def accumulate(block_index, totals):
        owner_expert = jnp.sum((block_starts <= block_index).astype(jnp.int32)) - 1
        within = ((block_index - block_starts[owner_expert]) * block_rows + jnp.arange(block_rows)).astype(jnp.int32)
        usable = within < counts[owner_expert]
        where_pair = sorted_pairs[jnp.clip(starts[owner_expert] + within, 0, pair_count - 1)]
        tokens = token_of[where_pair]
        gathered = moe_in[tokens]
        both_halves = jnp.dot(gathered, expert_in[owner_expert], preferred_element_type=jnp.float32)
        acted = (jax.nn.silu(both_halves[:, :FFE]) * both_halves[:, FFE:]).astype(jnp.bfloat16)
        result = jnp.dot(acted, expert_out[owner_expert], preferred_element_type=jnp.float32).astype(jnp.bfloat16)
        weight = jnp.where(usable, flat_shares[where_pair], 0.0)
        return totals.at[tokens].add(result.astype(jnp.float32) * weight[:, None])
    return lax.fori_loop(0, block_total, accumulate, jnp.zeros((pair_count // TOP, D), jnp.float32))

def reference(residual_in, query_in, key_in, value_in, gate_in, log_decay, write_rate, state_start, head_gain, out_proj, moe_gain, expert_in, expert_out, route_ids, route_probs):
    heads_out = delta_layer(query_in, key_in, value_in, log_decay, write_rate, state_start)
    normed = heads_out * lax.rsqrt(lax.optimization_barrier(jnp.mean(heads_out * heads_out, axis=-1, keepdims=True)) + 1e-06)
    normed = normed * head_gain * jax.nn.silu(gate_in.astype(jnp.float32).reshape(SEQUENCE_COUNT, WINDOW_LENGTH, H, DV))
    mixed = normed.astype(jnp.bfloat16).reshape(SEQUENCE_COUNT * WINDOW_LENGTH, H * DV)
    hidden = residual_in.astype(jnp.float32).reshape(SEQUENCE_COUNT * WINDOW_LENGTH, D) + jnp.dot(mixed, out_proj, preferred_element_type=jnp.float32)
    moe_in = (hidden * lax.rsqrt(lax.optimization_barrier(jnp.mean(hidden * hidden, axis=-1, keepdims=True)) + 1e-06) * moe_gain).astype(jnp.bfloat16)
    shares = route_probs / lax.optimization_barrier(jnp.sum(route_probs, axis=-1, keepdims=True))
    moe_total = expert_layer(moe_in, expert_in, expert_out, route_ids, shares)
    return (hidden + moe_total).astype(jnp.bfloat16).reshape(SEQUENCE_COUNT, WINDOW_LENGTH, D)
```

```python
import jax
import jax.numpy as jnp
from jax import lax
from jax.experimental import pallas as pl
from jax.experimental.pallas import tpu as pltpu
from jax.sharding import PartitionSpec as P

DK = 128
GROUP = 64
TOP = 10


HIGHEST = lax.Precision.HIGHEST


def entering(shard, axis, combine, identity):
    size, position = (lax.axis_size(axis), lax.axis_index(axis))
    everything = jax.tree.map(
        lambda part, kind: lax.all_gather(part.astype(kind), axis),
        shard,
        (jnp.bfloat16, jnp.bfloat16),
    )
    start = jax.tree.map(
        lambda part, zero: jnp.broadcast_to(jnp.asarray(zero, part.dtype), part.shape),
        shard,
        identity,
    )

    def hop(k, before):
        reached = k < position
        new = combine(
            before, jax.tree.map(lambda part, own: part[k].astype(own.dtype), everything, shard)
        )
        return jax.tree.map(lambda a, b: jnp.where(reached, a, b), new, before)

    return lax.fori_loop(0, size, hop, start)


def product(form, left, right):
    return jnp.einsum(form, left, right, precision=HIGHEST)


def unit_rows(values):
    return values * lax.rsqrt(jnp.sum(values * values, axis=-1, keepdims=True) + 1e-06)


def group_terms(query_rows, key_rows, value_rows, log_gates, strengths):
    length = log_gates.shape[-1]
    cumulative = jnp.cumsum(log_gates, axis=-1)
    log_gaps = cumulative[..., :, None] - cumulative[..., None, :]
    row_index = jnp.arange(length)[:, None]
    col_index = jnp.arange(length)[None, :]
    inclusive = col_index <= row_index
    strict = col_index < row_index
    decays = jnp.where(inclusive, jnp.exp(jnp.where(inclusive, log_gaps, 0.0)), 0.0)
    identity_c = jnp.eye(length, dtype=jnp.float32)
    identity_k = jnp.eye(key_rows.shape[-1], dtype=jnp.float32)
    couple = jnp.where(
        strict,
        strengths[..., :, None] * decays * product("...id,...jd->...ij", key_rows, key_rows),
        0.0,
    )
    inverse = identity_c - couple
    powers = couple
    extent = 2
    while extent < length:
        powers = product("...ij,...jk->...ik", powers, powers)
        inverse = product("...ij,...jk->...ik", inverse, identity_c + powers)
        extent = extent * 2
    gammas = jnp.exp(cumulative)
    pseudo = product("...ij,...jv->...iv", inverse, strengths[..., None] * value_rows)
    erased = product("...ij,...jd->...id", inverse, (strengths * gammas)[..., None] * key_rows)
    to_end = jnp.exp(cumulative[..., -1:] - cumulative)[..., None] * key_rows
    transfer = gammas[..., -1][..., None, None] * identity_k - product(
        "...ci,...cj->...ij", to_end, erased
    )
    offset = product("...ci,...cv->...iv", to_end, pseudo)
    scores = decays * product("...id,...jd->...ij", query_rows, key_rows)
    local_out = product("...ij,...jv->...iv", scores, pseudo)
    reach_map = gammas[..., None] * query_rows - product("...ij,...jd->...id", scores, erased)
    return (transfer, offset, local_out, reach_map)


def chain_combine(earlier, later):
    earlier_map, earlier_add = earlier
    later_map, later_add = later
    return (
        product("hij,hjk->hik", later_map, earlier_map),
        product("hij,hjv->hiv", later_map, earlier_add) + later_add,
    )

MIB = 1024 * 1024
MESH = pl.DeviceIdType.MESH


def partners(ctx):
    core, col, row = (ctx % 2, (ctx // 2) % 2, ctx // 4)
    return (ctx + 1 - 2 * core, ctx + 2 - 4 * col, ctx + 4 - 8 * row)


def greet(ctx, seq, depth):
    sib, xn, yn = partners(ctx)
    barrier = pltpu.get_barrier_semaphore()
    for other in (sib, xn, yn):
        pl.semaphore_signal(barrier, inc=1, device_id=(other, seq), device_id_type=MESH)
    for d in range(1, depth):
        pl.semaphore_signal(
            barrier, inc=1, device_id=(ctx, (seq + d) % depth), device_id_type=MESH
        )
    pl.semaphore_wait(barrier, 3 + depth - 1)


def gather_kernel(depth, x_ref, out_ref, own_sem, send_sem, recv_sem):
    ctx, seq = (lax.axis_index("ctx"), lax.axis_index("seq"))
    sib, xn, yn = partners(ctx)
    diag = xn + yn - ctx
    half = x_ref.shape[0] // 2
    low, high = (pl.ds(0, half), pl.ds(half, half))
    everything = pl.ds(0, 2 * half)
    greet(ctx, seq, depth)
    sent = []

    def send(group, kind, src, dst, ctx_to, seq_to, recv_group=None):
        copy = pltpu.make_async_remote_copy(
            src_ref=src,
            dst_ref=dst,
            send_sem=send_sem.at[group, kind],
            recv_sem=recv_sem.at[group if recv_group is None else recv_group, kind],
            device_id=(ctx_to, seq_to),
            device_id_type=MESH,
        )
        copy.start()
        sent.append(copy)

    def arrived(group, kind, block, rows):
        pltpu.make_async_remote_copy(
            src_ref=out_ref.at[(seq + group) % depth, block, rows],
            dst_ref=out_ref.at[(seq + group) % depth, block, rows],
            send_sem=send_sem.at[group, kind],
            recv_sem=recv_sem.at[group, kind],
            device_id=(ctx, seq),
            device_id_type=MESH,
        ).wait_recv()

    own = pltpu.make_async_copy(x_ref, out_ref.at[seq, ctx], own_sem)
    own.start()
    for d in range(1, depth):
        send(depth + d, 0, x_ref, out_ref.at[seq, ctx], ctx, (seq + d) % depth, depth - d)

    def spread(group):
        src = x_ref if group == 0 else out_ref.at[(seq + group) % depth, ctx]
        dst = out_ref.at[(seq + group) % depth, ctx]
        send(group, 1, src, dst, xn, seq)
        send(group, 2, src, dst, yn, seq)
        send(group, 5, src, dst, sib, seq)

    def relay(group):
        z = (seq + group) % depth
        arrived(group, 1, xn, everything)
        part = out_ref.at[z, xn, low]
        send(group, 3, part, part, yn, seq)
        part = out_ref.at[z, xn]
        send(group, 6, part, part, sib, seq)
        arrived(group, 2, yn, everything)
        part = out_ref.at[z, yn, high]
        send(group, 4, part, part, xn, seq)
        part = out_ref.at[z, yn]
        send(group, 7, part, part, sib, seq)

    def pass_on(group):
        z = (seq + group) % depth
        arrived(group, 3, diag, low)
        arrived(group, 4, diag, high)
        part = out_ref.at[z, diag]
        send(group, 8, part, part, sib, seq)

    spread(0)
    order = [0] + [d for d in range(1, depth)]
    for place, group in enumerate(order):
        if group != 0:
            arrived(group, 0, ctx, everything)
            spread(group)
        if place >= 1:
            relay(order[place - 1])
        if place >= 2:
            pass_on(order[place - 2])
    relay(order[-1])
    if depth >= 2:
        pass_on(order[-2])
    pass_on(order[-1])
    for group in order:
        arrived(group, 5, sib, everything)
        arrived(group, 6, xn + sib - ctx, everything)
        arrived(group, 7, yn + sib - ctx, everything)
        arrived(group, 8, diag + sib - ctx, everything)
    for copy in sent:
        copy.wait_send()
    own.wait()


def gather_rows(rows, ctx_count, depth):
    return pl.pallas_call(
        lambda *refs: gather_kernel(depth, *refs),
        out_shape=jax.ShapeDtypeStruct((depth, ctx_count) + rows.shape, rows.dtype),
        in_specs=[pl.BlockSpec(memory_space=pl.ANY)],
        out_specs=pl.BlockSpec(memory_space=pl.ANY),
        scratch_shapes=[
            pltpu.SemaphoreType.DMA,
            pltpu.SemaphoreType.DMA((2 * depth, 9)),
            pltpu.SemaphoreType.DMA((depth, 9)),
        ],
        compiler_params=pltpu.CompilerParams(collective_id=0, has_side_effects=True),
        name="gather_rows",
    )(rows)


def add_rows(target, terms):
    rows = target.shape[0]

    @pl.loop(0, rows // 16)
    def _(i):
        at = pl.ds(pl.multiple_of(i * 16, 16), 16)
        total = terms[0][at, :].astype(jnp.float32)
        for term in terms[1:]:
            total = total + term[at, :].astype(jnp.float32)
        target[at, :] = total.astype(target.dtype)


def reduce_kernel(depth, part_ref, out_ref, mine, from_sib, from_x, from_y, x_half, y_half,
                  from_z, load_sem, send_sem, recv_sem):
    ctx, seq = (lax.axis_index("ctx"), lax.axis_index("seq"))
    sib, xn, yn = partners(ctx)
    diag = xn + yn - ctx
    half = out_ref.shape[0] // 2
    low, high = (pl.ds(0, half), pl.ds(half, half))
    across = sib - ctx
    order = [d for d in range(1, depth)] + [0]
    blocks = (diag, xn, yn, ctx)
    loads = {}
    for group in order:
        for i, block in enumerate(blocks):
            loads[group, i] = pltpu.make_async_copy(
                part_ref.at[(seq + group) % depth, block], mine.at[group, i], load_sem.at[group, i]
            )
            loads[group, i].start()
    greet(ctx, seq, depth)
    started = {}

    def make(group, kind, src, dst, ctx_to, seq_to, recv_group=None):
        return pltpu.make_async_remote_copy(
            src_ref=src,
            dst_ref=dst,
            send_sem=send_sem.at[group, kind],
            recv_sem=recv_sem.at[group if recv_group is None else recv_group, kind],
            device_id=(ctx_to, seq_to),
            device_id_type=MESH,
        )

    def send(group, kind, *rest):
        copy = make(group, kind, *rest)
        copy.start()
        started[group, kind] = copy

    for group in order:
        z = (seq + group) % depth
        for i, block in enumerate(blocks):
            send(group, i, part_ref.at[z, block + across], from_sib.at[group, i], sib, seq)

    def first(group):
        for i in range(4):
            loads[group, i].wait()
            started[group, i].wait_recv()
            add_rows(mine.at[group, i], (mine.at[group, i], from_sib.at[group, i]))
            if i == 0:
                send(group, 4, mine.at[group, 0, low], x_half.at[group], yn, seq)
                send(group, 5, mine.at[group, 0, high], y_half.at[group], xn, seq)

    def second(group):
        started[group, 4].wait_recv()
        here = mine.at[group, 1, low]
        add_rows(here, (here, x_half.at[group]))
        send(group, 6, mine.at[group, 1], from_x.at[group], xn, seq)
        started[group, 5].wait_recv()
        here = mine.at[group, 2, high]
        add_rows(here, (here, y_half.at[group]))
        send(group, 7, mine.at[group, 2], from_y.at[group], yn, seq)

    def third(group):
        started[group, 6].wait_recv()
        started[group, 7].wait_recv()
        here = mine.at[group, 3]
        add_rows(here, (here, from_x.at[group], from_y.at[group]))
        if group != 0:
            send(group, 8, here, from_z.at[depth - group], ctx, (seq + group) % depth,
                 depth - group)

    first(order[0])
    for place, group in enumerate(order):
        if place + 1 < depth:
            first(order[place + 1])
        second(group)
        if place >= 1:
            third(order[place - 1])
    third(order[-1])
    for group in range(1, depth):
        make(group, 8, from_z.at[group], from_z.at[group], ctx, seq).wait_recv()
    add_rows(out_ref, [mine.at[0, 3]] + [from_z.at[d] for d in range(1, depth)])
    for copy in started.values():
        copy.wait_send()


def reduce_rows(parts):
    depth, ctx_count, rows, width = parts.shape
    kind = parts.dtype
    return pl.pallas_call(
        lambda *refs: reduce_kernel(depth, *refs),
        out_shape=jax.ShapeDtypeStruct((rows, width), jnp.float32),
        in_specs=[pl.BlockSpec(memory_space=pl.ANY)],
        out_specs=pl.BlockSpec(memory_space=pltpu.VMEM),
        scratch_shapes=[
            pltpu.VMEM((depth, 4, rows, width), kind),
            pltpu.VMEM((depth, 4, rows, width), kind),
            pltpu.VMEM((depth, rows, width), kind),
            pltpu.VMEM((depth, rows, width), kind),
            pltpu.VMEM((depth, rows // 2, width), kind),
            pltpu.VMEM((depth, rows // 2, width), kind),
            pltpu.VMEM((depth, rows, width), kind),
            pltpu.SemaphoreType.DMA((depth, 4)),
            pltpu.SemaphoreType.DMA((depth, 9)),
            pltpu.SemaphoreType.DMA((depth, 9)),
        ],
        compiler_params=pltpu.CompilerParams(
            collective_id=1, has_side_effects=True, vmem_limit_bytes=56 * MIB
        ),
        name="reduce_rows",
    )(parts)


def expert_kernel(x_ref, pick_ref, weight_ref, win_ref, wout_ref, out_ref, rows, acted, scaled):
    sources, capacity = (x_ref.shape[1], pick_ref.shape[3])
    experts, inner = (win_ref.shape[0], wout_ref.shape[1])
    tile = 256
    dot = lambda a, b: jnp.dot(a, b, preferred_element_type=jnp.float32)

    @pl.loop(0, sources)
    def _(s):
        for j in range(experts):
            at = pl.ds(pl.multiple_of(s * capacity, 16), capacity)
            rows[j, at, :] = dot(pick_ref[0, s, j], x_ref[0, s]).astype(jnp.bfloat16)

    @pl.loop(0, experts)
    def _(j):
        @pl.loop(0, inner // tile)
        def _(n):
            at = pl.ds(pl.multiple_of(n * tile, tile), tile)
            up_at = pl.ds(pl.multiple_of(inner + n * tile, tile), tile)
            gate = dot(rows[j], win_ref[j, :, at])
            up = dot(rows[j], win_ref[j, :, up_at])
            acted[:, at] = (gate / (1.0 + jnp.exp(-gate)) * up).astype(jnp.bfloat16)

        @pl.loop(0, x_ref.shape[3] // tile)
        def _(n):
            at = pl.ds(pl.multiple_of(n * tile, tile), tile)
            scaled[j, :, at] = (dot(acted[...], wout_ref[j, :, at]) * weight_ref[0, j]).astype(
                jnp.bfloat16
            )

    @pl.loop(0, sources)
    def _(s):
        at = pl.ds(pl.multiple_of(s * capacity, 16), capacity)
        total = 0.0
        for j in range(experts):
            total = total + lax.dot_general(
                pick_ref[0, s, j],
                scaled[j, at, :],
                (((0,), (0,)), ((), ())),
                preferred_element_type=jnp.float32,
            )
        out_ref[0, s] = total.astype(jnp.bfloat16)


def expert_rows(gathered, picks, weights, expert_in, expert_out):
    depth, sources, tokens, width = gathered.shape
    experts, capacity = picks.shape[2:4]
    inner = expert_out.shape[1]
    block = lambda shape: pl.BlockSpec((1,) + shape[1:], lambda g: (g,) + (0,) * (len(shape) - 1))
    return pl.pallas_call(
        expert_kernel,
        out_shape=jax.ShapeDtypeStruct(gathered.shape, jnp.bfloat16),
        grid=(depth,),
        in_specs=[
            block(gathered.shape),
            block(picks.shape),
            block(weights.shape),
            pl.BlockSpec(memory_space=pltpu.VMEM),
            pl.BlockSpec(memory_space=pltpu.VMEM),
        ],
        out_specs=block(gathered.shape),
        scratch_shapes=[
            pltpu.VMEM((experts, sources * capacity, width), jnp.bfloat16),
            pltpu.VMEM((sources * capacity, inner), jnp.bfloat16),
            pltpu.VMEM((experts, sources * capacity, width), jnp.bfloat16),
        ],
        compiler_params=pltpu.CompilerParams(vmem_limit_bytes=58 * MIB),
        name="expert_rows",
    )(gathered, picks, weights, expert_in, expert_out)


def picks_of(route_ids, shares, local_experts, capacity):
    ids = lax.all_gather(lax.all_gather(route_ids, "ctx"), "seq")
    parts = lax.all_gather(lax.all_gather(shares, "ctx"), "seq")
    first = (lax.axis_index("ctx") * lax.axis_size("seq") + lax.axis_index("seq")) * local_experts
    experts = first + jnp.arange(local_experts, dtype=jnp.int32)
    named = ids[:, :, None] == experts[:, None, None]
    weight = jnp.sum(jnp.where(named, parts[:, :, None], 0.0), axis=-1)
    named = jnp.any(named, axis=-1)
    tokens = ids.shape[2]
    earlier = (jnp.arange(tokens)[:, None] < jnp.arange(tokens)[None, :]).astype(jnp.bfloat16)
    slot = jnp.einsum(
        "zcjt,tu->zcju", named.astype(jnp.bfloat16), earlier, preferred_element_type=jnp.float32
    ).astype(jnp.int32)
    picks = named[..., None, :] & (slot[..., None, :] == jnp.arange(capacity)[:, None])
    slot_weight = jnp.sum(jnp.where(picks, weight[..., None, :], 0.0), axis=-1)
    depth, ctx_count = ids.shape[:2]
    slot_weight = slot_weight.transpose(0, 2, 1, 3).reshape(
        depth, local_experts, ctx_count * capacity, 1
    )
    return (picks.astype(jnp.bfloat16), slot_weight)


def apply_experts(arrived, expert_in, expert_out):
    inner_width = expert_out.shape[1]
    both_halves = jnp.einsum(
        "sjnd,jdf->sjnf", arrived, expert_in, preferred_element_type=jnp.float32
    )
    acted = (jax.nn.silu(both_halves[..., :inner_width]) * both_halves[..., inner_width:]).astype(
        jnp.bfloat16
    )
    return jnp.einsum(
        "sjnf,jfd->sjnd", acted, expert_out, preferred_element_type=jnp.float32
    ).astype(jnp.bfloat16)


def local(
    residual_in,
    query_in,
    key_in,
    value_in,
    gate_in,
    log_decay,
    write_rate,
    state_start,
    head_gain,
    out_proj,
    moe_gain,
    expert_in,
    expert_out,
    route_ids,
    route_probs,
):
    tokens_here = residual_in.shape[1]
    model_width = residual_in.shape[2]
    heads_all = log_decay.shape[1]
    key_heads = query_in.shape[2] // DK
    value_size = value_in.shape[2] // heads_all
    repeat_by = heads_all // key_heads
    group_count = tokens_here // GROUP
    queries = unit_rows(query_in[0].astype(jnp.float32).reshape(tokens_here, key_heads, DK))
    queries = (
        jnp.repeat(queries, repeat_by, axis=1)
        .transpose(1, 0, 2)
        .reshape(heads_all, group_count, GROUP, DK)
    )
    key_rows = unit_rows(key_in[0].astype(jnp.float32).reshape(tokens_here, key_heads, DK))
    key_rows = (
        jnp.repeat(key_rows, repeat_by, axis=1)
        .transpose(1, 0, 2)
        .reshape(heads_all, group_count, GROUP, DK)
    )
    value_rows = (
        value_in[0]
        .astype(jnp.float32)
        .reshape(tokens_here, heads_all, value_size)
        .transpose(1, 0, 2)
    )
    value_rows = value_rows.reshape(heads_all, group_count, GROUP, value_size)
    gates = log_decay[0].reshape(heads_all, group_count, GROUP)
    strengths = write_rate[0].reshape(heads_all, group_count, GROUP)
    transfer, offset, local_out, reach_map = group_terms(
        queries, key_rows, value_rows, gates, strengths
    )
    identity_k = jnp.broadcast_to(jnp.eye(DK, dtype=jnp.float32), (heads_all, DK, DK))
    empty_add = jnp.zeros((heads_all, DK, value_size), jnp.float32)

    def compose(carried, pieces):
        total_map, total_add = carried
        step_map, step_add, step_local, step_reach = pieces
        joined_reach = product("hcd,hde->hce", step_reach, total_map)
        joined_local = step_local + product("hcd,hdv->hcv", step_reach, total_add)
        total_map = product("hij,hjk->hik", step_map, total_map)
        total_add = product("hij,hjv->hiv", step_map, total_add) + step_add
        return ((total_map, total_add), (joined_local, joined_reach))

    (block_map, block_add), (joined_local, joined_reach) = lax.scan(
        compose,
        (identity_k, empty_add),
        (
            jnp.moveaxis(transfer, 1, 0),
            jnp.moveaxis(offset, 1, 0),
            jnp.moveaxis(local_out, 1, 0),
            jnp.moveaxis(reach_map, 1, 0),
        ),
    )
    start_state = state_start[0]
    prior_map, prior_add = entering(
        (block_map, block_add), "ctx", chain_combine, (identity_k, empty_add)
    )
    state_in = product("hij,hjv->hiv", prior_map, start_state) + prior_add
    heads_out = joined_local + product("nhcd,hdv->nhcv", joined_reach, state_in)
    heads_out = heads_out.transpose(0, 2, 1, 3).reshape(tokens_here, heads_all, value_size)
    normed = heads_out * lax.rsqrt(jnp.mean(heads_out * heads_out, axis=-1, keepdims=True) + 1e-06)
    normed = (
        normed
        * head_gain
        * jax.nn.silu(gate_in[0].astype(jnp.float32).reshape(tokens_here, heads_all, value_size))
    )
    mixed = normed.astype(jnp.bfloat16).reshape(tokens_here, heads_all * value_size)
    hidden = residual_in[0].astype(jnp.float32) + jnp.dot(
        mixed, out_proj, preferred_element_type=jnp.float32
    )
    moe_in = (
        hidden * lax.rsqrt(jnp.mean(hidden * hidden, axis=-1, keepdims=True) + 1e-06) * moe_gain
    ).astype(jnp.bfloat16)
    shares = route_probs[0] / jnp.sum(route_probs[0], axis=-1, keepdims=True)
    ctx_count = lax.axis_size("ctx")
    seq_count = lax.axis_size("seq")
    local_experts = expert_in.shape[0]
    experts_all = local_experts * ctx_count * seq_count
    capacity = max(2, 12 * tokens_here * TOP // (5 * experts_all))
    if ctx_count == 8 and seq_count > 1 and capacity % 16 == 0:
        picks, slot_weight = picks_of(route_ids[0], shares, local_experts, capacity)
        gathered = gather_rows(moe_in, ctx_count, seq_count)
        partial = expert_rows(gathered, picks, slot_weight, expert_in, expert_out)
        return (hidden + reduce_rows(partial)).astype(jnp.bfloat16)[None]
    flat_ids = route_ids[0].reshape(-1)
    pair_count = flat_ids.shape[0]
    pair_order = jnp.arange(pair_count, dtype=jnp.int32)
    token_of = pair_order // TOP
    earlier_pair = pair_order[None, :] < pair_order[:, None]
    slot_index = jnp.sum(
        ((flat_ids[None, :] == flat_ids[:, None]) & earlier_pair).astype(jnp.int32), axis=1
    )
    target = flat_ids * capacity + slot_index
    outbound = (
        jnp.zeros((experts_all * capacity, model_width), jnp.bfloat16)
        .at[target]
        .set(moe_in[token_of])
    )
    shaped = outbound.reshape(ctx_count * seq_count, local_experts, capacity, model_width)
    returned = lax.all_to_all(
        apply_experts(
            lax.all_to_all(shaped, ("ctx", "seq"), split_axis=0, concat_axis=0, tiled=True),
            expert_in,
            expert_out,
        ),
        ("ctx", "seq"),
        split_axis=0,
        concat_axis=0,
        tiled=True,
    )
    back_rows = returned.reshape(experts_all * capacity, model_width)[target]
    back_rows = back_rows.reshape(tokens_here, TOP, model_width)
    moe_total = jnp.einsum("tkd,tk->td", back_rows.astype(jnp.float32), shares)
    return (hidden + moe_total).astype(jnp.bfloat16)[None]


def solution(mesh):
    in_specs = (
        P("seq", "ctx", None),
        P("seq", "ctx", None),
        P("seq", "ctx", None),
        P("seq", "ctx", None),
        P("seq", "ctx", None),
        P("seq", None, "ctx"),
        P("seq", None, "ctx"),
        P("seq", None, None, None),
        P(),
        P(),
        P(),
        P(("ctx", "seq"), None, None),
        P(("ctx", "seq"), None, None),
        P("seq", "ctx", None),
        P("seq", "ctx", None),
    )
    out_specs = P("seq", "ctx", None)
    return jax.shard_map(local, mesh=mesh, in_specs=in_specs, out_specs=out_specs, check_vma=False)
```

```python
import jax
import jax.numpy as jnp
from jax import lax
from jax.experimental import pallas as pl
from jax.experimental.pallas import tpu as pltpu
from jax.sharding import PartitionSpec as P

DK = 128
GROUP = 64
TOP = 10


HIGHEST = lax.Precision.HIGHEST


def entering(shard, axis, combine, identity):
    size, position = (lax.axis_size(axis), lax.axis_index(axis))
    everything = jax.tree.map(
        lambda part, kind: lax.all_gather(part.astype(kind), axis),
        shard,
        (jnp.bfloat16, jnp.bfloat16),
    )
    start = jax.tree.map(
        lambda part, zero: jnp.broadcast_to(jnp.asarray(zero, part.dtype), part.shape),
        shard,
        identity,
    )

    def hop(k, before):
        reached = k < position
        new = combine(
            before, jax.tree.map(lambda part, own: part[k].astype(own.dtype), everything, shard)
        )
        return jax.tree.map(lambda a, b: jnp.where(reached, a, b), new, before)

    return lax.fori_loop(0, size, hop, start)


def product(form, left, right):
    return jnp.einsum(form, left, right, precision=HIGHEST)


def unit_rows(values):
    return values * lax.rsqrt(jnp.sum(values * values, axis=-1, keepdims=True) + 1e-06)


def group_terms(query_rows, key_rows, value_rows, log_gates, strengths):
    length = log_gates.shape[-1]
    cumulative = jnp.cumsum(log_gates, axis=-1)
    log_gaps = cumulative[..., :, None] - cumulative[..., None, :]
    row_index = jnp.arange(length)[:, None]
    col_index = jnp.arange(length)[None, :]
    inclusive = col_index <= row_index
    strict = col_index < row_index
    decays = jnp.where(inclusive, jnp.exp(jnp.where(inclusive, log_gaps, 0.0)), 0.0)
    identity_c = jnp.eye(length, dtype=jnp.float32)
    identity_k = jnp.eye(key_rows.shape[-1], dtype=jnp.float32)
    couple = jnp.where(
        strict,
        strengths[..., :, None] * decays * product("...id,...jd->...ij", key_rows, key_rows),
        0.0,
    )
    inverse = identity_c - couple
    powers = couple
    extent = 2
    while extent < length:
        powers = product("...ij,...jk->...ik", powers, powers)
        inverse = product("...ij,...jk->...ik", inverse, identity_c + powers)
        extent = extent * 2
    gammas = jnp.exp(cumulative)
    pseudo = product("...ij,...jv->...iv", inverse, strengths[..., None] * value_rows)
    erased = product("...ij,...jd->...id", inverse, (strengths * gammas)[..., None] * key_rows)
    to_end = jnp.exp(cumulative[..., -1:] - cumulative)[..., None] * key_rows
    transfer = gammas[..., -1][..., None, None] * identity_k - product(
        "...ci,...cj->...ij", to_end, erased
    )
    offset = product("...ci,...cv->...iv", to_end, pseudo)
    scores = decays * product("...id,...jd->...ij", query_rows, key_rows)
    local_out = product("...ij,...jv->...iv", scores, pseudo)
    reach_map = gammas[..., None] * query_rows - product("...ij,...jd->...id", scores, erased)
    return (transfer, offset, local_out, reach_map)


def chain_combine(earlier, later):
    earlier_map, earlier_add = earlier
    later_map, later_add = later
    return (
        product("hij,hjk->hik", later_map, earlier_map),
        product("hij,hjv->hiv", later_map, earlier_add) + later_add,
    )

MIB = 1024 * 1024
MESH = pl.DeviceIdType.MESH


def partners(ctx):
    core, col, row = (ctx % 2, (ctx // 2) % 2, ctx // 4)
    return (ctx + 1 - 2 * core, ctx + 2 - 4 * col, ctx + 4 - 8 * row)


def greet(ctx, seq, depth):
    sib, xn, yn = partners(ctx)
    barrier = pltpu.get_barrier_semaphore()
    for other in (sib, xn, yn):
        pl.semaphore_signal(barrier, inc=1, device_id=(other, seq), device_id_type=MESH)
    for d in range(1, depth):
        pl.semaphore_signal(
            barrier, inc=1, device_id=(ctx, (seq + d) % depth), device_id_type=MESH
        )
    pl.semaphore_wait(barrier, 3 + depth - 1)


def add_rows(target, terms):
    rows = target.shape[0]

    @pl.loop(0, rows // 16)
    def _(i):
        at = pl.ds(pl.multiple_of(i * 16, 16), 16)
        total = terms[0][at, :].astype(jnp.float32)
        for term in terms[1:]:
            total = total + term[at, :].astype(jnp.float32)
        target[at, :] = total.astype(target.dtype)


def apply_picked(z, x_ref, pick_ref, weight_ref, win_ref, wout_ref, rows, acted, part):
    sources = x_ref.shape[0]
    experts, inner = (win_ref.shape[0], wout_ref.shape[1])
    capacity = pick_ref.shape[2] // experts
    tile = 256
    dot = lambda a, b: jnp.dot(a, b, preferred_element_type=jnp.float32)

    @pl.loop(0, sources)
    def _(s):
        at = pl.ds(pl.multiple_of(s * capacity, 16), capacity)
        picked = dot(pick_ref[z, s], x_ref[s]).astype(jnp.bfloat16)
        for j in range(experts):
            rows[j, at, :] = picked[j * capacity : (j + 1) * capacity]

    @pl.loop(0, experts)
    def _(j):
        @pl.loop(0, inner // tile)
        def _(n):
            at = pl.ds(pl.multiple_of(n * tile, tile), tile)
            up_at = pl.ds(pl.multiple_of(inner + n * tile, tile), tile)
            gate = dot(rows[j], win_ref[j, :, at])
            up = dot(rows[j], win_ref[j, :, up_at])
            acted[:, at] = (gate / (1.0 + jnp.exp(-gate)) * up).astype(jnp.bfloat16)

        @pl.loop(0, x_ref.shape[2] // tile)
        def _(n):
            at = pl.ds(pl.multiple_of(n * tile, tile), tile)
            rows[j, :, at] = (dot(acted[...], wout_ref[j, :, at]) * weight_ref[z, j]).astype(
                jnp.bfloat16
            )

    @pl.loop(0, sources)
    def _(s):
        at = pl.ds(pl.multiple_of(s * capacity, 16), capacity)
        both = jnp.concatenate([rows[j, at, :] for j in range(experts)], axis=0)
        part[s] = lax.dot_general(
            pick_ref[z, s],
            both,
            (((0,), (0,)), ((), ())),
            preferred_element_type=jnp.float32,
        ).astype(jnp.bfloat16)


def expert_kernel(depth, x_ref, pick_ref, weight_ref, win_hbm, wout_hbm, out_ref, all_ref,
                  win_ref, wout_ref, x_buf, rows, acted, part, from_sib, from_x, from_y,
                  x_half, y_half, from_z, own_sem, load_sem, gsend, grecv, rsend, rrecv):
    ctx, seq = (lax.axis_index("ctx"), lax.axis_index("seq"))
    sib, xn, yn = partners(ctx)
    diag, across = (xn + yn - ctx, sib - ctx)
    half = x_ref.shape[0] // 2
    low, high = (pl.ds(0, half), pl.ds(half, half))
    everything = pl.ds(0, 2 * half)
    load_in = pltpu.make_async_copy(win_hbm, win_ref, own_sem.at[0])
    load_out = pltpu.make_async_copy(wout_hbm, wout_ref, own_sem.at[1])
    own = pltpu.make_async_copy(x_ref, all_ref.at[seq, ctx], own_sem.at[2])
    own.start()
    greet(ctx, seq, depth)
    sent = []

    def place_of(group):
        return (seq + group) % depth

    def remote(sems, group, kind, src, dst, ctx_to, seq_to, recv_group=None):
        return pltpu.make_async_remote_copy(
            src_ref=src,
            dst_ref=dst,
            send_sem=sems[0].at[group, kind],
            recv_sem=sems[1].at[group if recv_group is None else recv_group, kind],
            device_id=(ctx_to, seq_to),
            device_id_type=MESH,
        )

    def start(sems, *rest):
        copy = remote(sems, *rest)
        copy.start()
        sent.append(copy)

    gather, reduce = ((gsend, grecv), (rsend, rrecv))

    def landed(sems, group, kind, ref):
        remote(sems, group, kind, ref, ref, ctx, seq).wait_recv()

    def arrived(group, kind, block, span):
        landed(gather, group, kind, all_ref.at[place_of(group), block, span])

    def spread(group):
        if group != 0:
            arrived(group, 0, ctx, everything)
        dst = all_ref.at[place_of(group), ctx]
        src = x_ref if group == 0 else dst
        start(gather, group, 1, src, dst, xn, seq)
        start(gather, group, 2, src, dst, yn, seq)
        start(gather, group, 5, src, dst, sib, seq)

    def relay(group):
        z = place_of(group)
        arrived(group, 1, xn, everything)
        piece = all_ref.at[z, xn, low]
        start(gather, group, 3, piece, piece, yn, seq)
        piece = all_ref.at[z, xn]
        start(gather, group, 6, piece, piece, sib, seq)
        arrived(group, 2, yn, everything)
        piece = all_ref.at[z, yn, high]
        start(gather, group, 4, piece, piece, xn, seq)
        piece = all_ref.at[z, yn]
        start(gather, group, 7, piece, piece, sib, seq)

    def pass_on(group):
        arrived(group, 3, diag, low)
        arrived(group, 4, diag, high)
        piece = all_ref.at[place_of(group), diag]
        start(gather, group, 8, piece, piece, sib, seq)

    def compute(group):
        arrived(group, 5, sib, everything)
        arrived(group, 6, xn + across, everything)
        arrived(group, 7, yn + across, everything)
        arrived(group, 8, diag + across, everything)
        z = place_of(group)
        load = pltpu.make_async_copy(all_ref.at[z], x_buf, load_sem.at[group])
        load.start()
        load.wait()
        apply_picked(z, x_buf, pick_ref, weight_ref, win_ref, wout_ref, rows, acted,
                     part.at[group])
        for i, block in enumerate((diag, xn, yn, ctx)):
            start(reduce, group, i, part.at[group, block + across], from_sib.at[group, i], sib,
                  seq)

    def first(group):
        for i, block in enumerate((diag, xn, yn, ctx)):
            here = part.at[group, block]
            landed(reduce, group, i, from_sib.at[group, i])
            add_rows(here, (here, from_sib.at[group, i]))
            if i == 0:
                start(reduce, group, 4, part.at[group, diag, low], x_half.at[group], yn, seq)
                start(reduce, group, 5, part.at[group, diag, high], y_half.at[group], xn, seq)

    def second(group):
        landed(reduce, group, 4, x_half.at[group])
        here = part.at[group, xn, low]
        add_rows(here, (here, x_half.at[group]))
        start(reduce, group, 6, part.at[group, xn], from_x.at[group], xn, seq)
        landed(reduce, group, 5, y_half.at[group])
        here = part.at[group, yn, high]
        add_rows(here, (here, y_half.at[group]))
        start(reduce, group, 7, part.at[group, yn], from_y.at[group], yn, seq)

    def third(group):
        landed(reduce, group, 6, from_x.at[group])
        landed(reduce, group, 7, from_y.at[group])
        here = part.at[group, ctx]
        add_rows(here, (here, from_x.at[group], from_y.at[group]))
        if group != 0:
            start(reduce, group, 8, here, from_z.at[depth - group], ctx, place_of(group),
                  depth - group)

    for d in range(1, depth):
        start(gather, depth + d, 0, x_ref, all_ref.at[seq, ctx], ctx, place_of(d), depth - d)
    spread(0)
    load_in.start()
    load_out.start()
    order = [d for d in range(1, depth)] + [0]
    spread(1)
    relay(0)
    spread(2)
    pass_on(0)
    relay(1)
    spread(3)
    pass_on(1)
    relay(2)
    own.wait()
    load_in.wait()
    load_out.wait()
    compute(1)
    pass_on(2)
    relay(3)
    first(1)
    compute(2)
    pass_on(3)
    second(1)
    first(2)
    compute(3)
    third(1)
    second(2)
    first(3)
    compute(0)
    third(2)
    second(3)
    first(0)
    third(3)
    second(0)
    third(0)
    for group in range(1, depth):
        landed(reduce, group, 8, from_z.at[group])
    add_rows(out_ref, [part.at[0, ctx]] + [from_z.at[d] for d in range(1, depth)])
    for copy in sent:
        copy.wait_send()


def routed_rows(rows_in, picks, weights, expert_in, expert_out, ctx_count, depth):
    tokens, width = rows_in.shape
    kind = rows_in.dtype
    experts, inner = expert_out.shape[:2]
    slots = weights.shape[2]
    vmem = pl.BlockSpec(memory_space=pltpu.VMEM)
    hbm = pl.BlockSpec(memory_space=pl.ANY)
    return pl.pallas_call(
        lambda *refs: expert_kernel(depth, *refs),
        out_shape=(
            jax.ShapeDtypeStruct((tokens, width), jnp.float32),
            jax.ShapeDtypeStruct((depth, ctx_count, tokens, width), kind),
        ),
        in_specs=[hbm, vmem, vmem, hbm, hbm],
        out_specs=(vmem, hbm),
        scratch_shapes=[
            pltpu.VMEM(expert_in.shape, kind),
            pltpu.VMEM(expert_out.shape, kind),
            pltpu.VMEM((ctx_count, tokens, width), kind),
            pltpu.VMEM((experts, slots, width), kind),
            pltpu.VMEM((slots, inner), kind),
            pltpu.VMEM((depth, ctx_count, tokens, width), kind),
            pltpu.VMEM((depth, 4, tokens, width), kind),
            pltpu.VMEM((depth, tokens, width), kind),
            pltpu.VMEM((depth, tokens, width), kind),
            pltpu.VMEM((depth, tokens // 2, width), kind),
            pltpu.VMEM((depth, tokens // 2, width), kind),
            pltpu.VMEM((depth, tokens, width), kind),
            pltpu.SemaphoreType.DMA((3,)),
            pltpu.SemaphoreType.DMA((depth,)),
            pltpu.SemaphoreType.DMA((2 * depth, 9)),
            pltpu.SemaphoreType.DMA((depth, 9)),
            pltpu.SemaphoreType.DMA((depth, 9)),
            pltpu.SemaphoreType.DMA((depth, 9)),
        ],
        compiler_params=pltpu.CompilerParams(
            collective_id=0, has_side_effects=True, vmem_limit_bytes=62 * MIB
        ),
        name="routed_rows",
    )(rows_in, picks, weights, expert_in, expert_out)[0]


def picks_of(route_ids, shares, local_experts, capacity):
    both = jnp.concatenate([route_ids.astype(jnp.float32), shares], axis=1).T
    both = lax.all_gather(both, ("seq", "ctx"))
    both = both.reshape((lax.axis_size("seq"), lax.axis_size("ctx")) + both.shape[1:])
    both = both.transpose(0, 1, 3, 2)
    ids = both[..., : route_ids.shape[1]].astype(jnp.int32)
    parts = both[..., route_ids.shape[1] :]
    first = (lax.axis_index("ctx") * lax.axis_size("seq") + lax.axis_index("seq")) * local_experts
    experts = first + jnp.arange(local_experts, dtype=jnp.int32)
    named = ids[:, :, None] == experts[:, None, None]
    weight = jnp.sum(jnp.where(named, parts[:, :, None], 0.0), axis=-1)
    named = jnp.any(named, axis=-1)
    tokens = ids.shape[2]
    earlier = (jnp.arange(tokens)[:, None] < jnp.arange(tokens)[None, :]).astype(jnp.bfloat16)
    slot = jnp.einsum(
        "zcjt,tu->zcju", named.astype(jnp.bfloat16), earlier, preferred_element_type=jnp.float32
    ).astype(jnp.int32)
    picks = named[..., None, :] & (slot[..., None, :] == jnp.arange(capacity)[:, None])
    slot_weight = jnp.sum(jnp.where(picks, weight[..., None, :], 0.0), axis=-1)
    depth, ctx_count = ids.shape[:2]
    slot_weight = slot_weight.transpose(0, 2, 1, 3).reshape(
        depth, local_experts, ctx_count * capacity, 1
    )
    picks = picks.reshape(depth, ctx_count, local_experts * capacity, tokens)
    return (picks.astype(jnp.bfloat16), slot_weight)


def apply_experts(arrived, expert_in, expert_out):
    inner_width = expert_out.shape[1]
    both_halves = jnp.einsum(
        "sjnd,jdf->sjnf", arrived, expert_in, preferred_element_type=jnp.float32
    )
    acted = (jax.nn.silu(both_halves[..., :inner_width]) * both_halves[..., inner_width:]).astype(
        jnp.bfloat16
    )
    return jnp.einsum(
        "sjnf,jfd->sjnd", acted, expert_out, preferred_element_type=jnp.float32
    ).astype(jnp.bfloat16)


def local(
    residual_in,
    query_in,
    key_in,
    value_in,
    gate_in,
    log_decay,
    write_rate,
    state_start,
    head_gain,
    out_proj,
    moe_gain,
    expert_in,
    expert_out,
    route_ids,
    route_probs,
):
    tokens_here = residual_in.shape[1]
    model_width = residual_in.shape[2]
    heads_all = log_decay.shape[1]
    key_heads = query_in.shape[2] // DK
    value_size = value_in.shape[2] // heads_all
    repeat_by = heads_all // key_heads
    group_count = tokens_here // GROUP
    queries = unit_rows(query_in[0].astype(jnp.float32).reshape(tokens_here, key_heads, DK))
    queries = (
        jnp.repeat(queries, repeat_by, axis=1)
        .transpose(1, 0, 2)
        .reshape(heads_all, group_count, GROUP, DK)
    )
    key_rows = unit_rows(key_in[0].astype(jnp.float32).reshape(tokens_here, key_heads, DK))
    key_rows = (
        jnp.repeat(key_rows, repeat_by, axis=1)
        .transpose(1, 0, 2)
        .reshape(heads_all, group_count, GROUP, DK)
    )
    value_rows = (
        value_in[0]
        .astype(jnp.float32)
        .reshape(tokens_here, heads_all, value_size)
        .transpose(1, 0, 2)
    )
    value_rows = value_rows.reshape(heads_all, group_count, GROUP, value_size)
    gates = log_decay[0].reshape(heads_all, group_count, GROUP)
    strengths = write_rate[0].reshape(heads_all, group_count, GROUP)
    transfer, offset, local_out, reach_map = group_terms(
        queries, key_rows, value_rows, gates, strengths
    )
    identity_k = jnp.broadcast_to(jnp.eye(DK, dtype=jnp.float32), (heads_all, DK, DK))
    empty_add = jnp.zeros((heads_all, DK, value_size), jnp.float32)

    def compose(carried, pieces):
        total_map, total_add = carried
        step_map, step_add, step_local, step_reach = pieces
        joined_reach = product("hcd,hde->hce", step_reach, total_map)
        joined_local = step_local + product("hcd,hdv->hcv", step_reach, total_add)
        total_map = product("hij,hjk->hik", step_map, total_map)
        total_add = product("hij,hjv->hiv", step_map, total_add) + step_add
        return ((total_map, total_add), (joined_local, joined_reach))

    (block_map, block_add), (joined_local, joined_reach) = lax.scan(
        compose,
        (identity_k, empty_add),
        (
            jnp.moveaxis(transfer, 1, 0),
            jnp.moveaxis(offset, 1, 0),
            jnp.moveaxis(local_out, 1, 0),
            jnp.moveaxis(reach_map, 1, 0),
        ),
    )
    start_state = state_start[0]
    prior_map, prior_add = entering(
        (block_map, block_add), "ctx", chain_combine, (identity_k, empty_add)
    )
    state_in = product("hij,hjv->hiv", prior_map, start_state) + prior_add
    heads_out = joined_local + product("nhcd,hdv->nhcv", joined_reach, state_in)
    heads_out = heads_out.transpose(0, 2, 1, 3).reshape(tokens_here, heads_all, value_size)
    normed = heads_out * lax.rsqrt(jnp.mean(heads_out * heads_out, axis=-1, keepdims=True) + 1e-06)
    normed = (
        normed
        * head_gain
        * jax.nn.silu(gate_in[0].astype(jnp.float32).reshape(tokens_here, heads_all, value_size))
    )
    mixed = normed.astype(jnp.bfloat16).reshape(tokens_here, heads_all * value_size)
    hidden = residual_in[0].astype(jnp.float32) + jnp.dot(
        mixed, out_proj, preferred_element_type=jnp.float32
    )
    moe_in = (
        hidden * lax.rsqrt(jnp.mean(hidden * hidden, axis=-1, keepdims=True) + 1e-06) * moe_gain
    ).astype(jnp.bfloat16)
    shares = route_probs[0] / jnp.sum(route_probs[0], axis=-1, keepdims=True)
    ctx_count = lax.axis_size("ctx")
    seq_count = lax.axis_size("seq")
    local_experts = expert_in.shape[0]
    experts_all = local_experts * ctx_count * seq_count
    capacity = max(2, 12 * tokens_here * TOP // (5 * experts_all))
    if ctx_count == 8 and seq_count == 4 and capacity % 16 == 0:
        picks, slot_weight = picks_of(route_ids[0], shares, local_experts, capacity)
        moe_total = routed_rows(
            moe_in, picks, slot_weight, expert_in, expert_out, ctx_count, seq_count
        )
        return (hidden + moe_total).astype(jnp.bfloat16)[None]
    flat_ids = route_ids[0].reshape(-1)
    pair_count = flat_ids.shape[0]
    pair_order = jnp.arange(pair_count, dtype=jnp.int32)
    token_of = pair_order // TOP
    earlier_pair = pair_order[None, :] < pair_order[:, None]
    slot_index = jnp.sum(
        ((flat_ids[None, :] == flat_ids[:, None]) & earlier_pair).astype(jnp.int32), axis=1
    )
    target = flat_ids * capacity + slot_index
    outbound = (
        jnp.zeros((experts_all * capacity, model_width), jnp.bfloat16)
        .at[target]
        .set(moe_in[token_of])
    )
    shaped = outbound.reshape(ctx_count * seq_count, local_experts, capacity, model_width)
    returned = lax.all_to_all(
        apply_experts(
            lax.all_to_all(shaped, ("ctx", "seq"), split_axis=0, concat_axis=0, tiled=True),
            expert_in,
            expert_out,
        ),
        ("ctx", "seq"),
        split_axis=0,
        concat_axis=0,
        tiled=True,
    )
    back_rows = returned.reshape(experts_all * capacity, model_width)[target]
    back_rows = back_rows.reshape(tokens_here, TOP, model_width)
    moe_total = jnp.einsum("tkd,tk->td", back_rows.astype(jnp.float32), shares)
    return (hidden + moe_total).astype(jnp.bfloat16)[None]


def solution(mesh):
    in_specs = (
        P("seq", "ctx", None),
        P("seq", "ctx", None),
        P("seq", "ctx", None),
        P("seq", "ctx", None),
        P("seq", "ctx", None),
        P("seq", None, "ctx"),
        P("seq", None, "ctx"),
        P("seq", None, None, None),
        P(),
        P(),
        P(),
        P(("ctx", "seq"), None, None),
        P(("ctx", "seq"), None, None),
        P("seq", "ctx", None),
        P("seq", "ctx", None),
    )
    out_specs = P("seq", "ctx", None)
    return jax.shard_map(local, mesh=mesh, in_specs=in_specs, out_specs=out_specs, check_vma=False)
```
